256 devices in a mesh: ctx: 8 (over z_hi, y), exp: 32 (over z_lo, x, core).
Axes of the slice: x: 4, y: 4, z: 8 (z_hi: 2, z_lo: 4; z = z_hi * 4 + z_lo), core: 2. Of those that a mesh axis runs over, the one named last changes fastest.
Arguments:
- query_rows: bfloat16 [32, 1024, 2048], P('exp', 'ctx'), may hold values from -5 to 5
- key_rows: bfloat16 [32, 1024, 256], P('exp', 'ctx'), may hold values from -5 to 5
- value_rows: bfloat16 [32, 1024, 256], P('exp', 'ctx'), may hold values from -6 to 6
- residual: bfloat16 [32, 1024, 2048], P('exp', None, 'ctx'), may hold values from -6 to 6
- out_weight: bfloat16 [2048, 2048], P(None, 'ctx'), may hold values from -0.125 to 0.125
- norm_gain: float32 [2048], P('ctx'), may hold values from 0.25 to 1.75
- gate_up: bfloat16 [256, 2048, 768], P(('ctx', 'exp')), may hold values from -0.125 to 0.125
- down_proj: bfloat16 [256, 384, 2048], P(('ctx', 'exp')), may hold values from -0.21875 to 0.21875
- expert_ids: int32 [32, 1024, 8], P('exp'), may hold values from 0 to 127, all different within a row; in each aligned block of 1024 rows (0 to 1023, 1024 to 2047, ..., all dimensions but the last counted through in order) at most 76 rows name the same one
- gate_vals: float32 [32, 1024, 8], P('exp'), may hold values from 0.02 to 0.3
Outputs:
- layer_out: bfloat16 [32, 1024, 2048], P('exp', None, 'ctx')
The draws below stay inside these ranges and needn't reach their ends.
Inputs may be any that keep to these rules, and one draw needn't show every extreme that they name: `expert_ids`: the entries of one position name different experts. In each sequence no expert is named by more than 76 entries, and in some sequence one expert is named by exactly 76.
All inputs are finite; a program needn't handle non-finite values.
Results may differ from the reference program's by a relative error of at most 0.009.
Values may be sent and summed in bfloat16 or wider, within the bound.
A program may use at most 128 MiB of HBM per device.

```python
import math
import jax
import jax.numpy as jnp
import numpy as np
from jax import lax

D = 2048
HEADS = 16
KV_HEADS = 2
HEAD = 128
FF = 768
TOP = 8
LENGTH = 1024
SEQS = 32
GROUP = 32
CLASSES = 4
EXPERTS = 128
HALF = 384
CAP = 76


def draw_query_rows(key, part):
    key = jax.random.fold_in(key, 3)
    drawn = jnp.clip(jax.random.normal(key, (SEQS, LENGTH, HEADS * HEAD), jnp.float32), -5.0, 5.0)
    return drawn.astype(jnp.bfloat16)


def draw_key_rows(key, part):
    key = jax.random.fold_in(key, 5)
    drawn = jnp.clip(jax.random.normal(key, (SEQS, LENGTH, KV_HEADS * HEAD), jnp.float32), -5.0, 5.0)
    return drawn.astype(jnp.bfloat16)


def shard_levels(own_key, shape, cuts, smallest, high):
    def one(axis_at, blocks):
        steps = jax.random.uniform(jax.random.fold_in(jax.random.fold_in(own_key, 6), axis_at), (blocks,), jnp.float32, smallest / len(cuts), high / len(cuts))
        return jnp.repeat(jnp.exp(steps), shape[axis_at] // blocks).reshape((-1,) + (1,) * (len(shape) - axis_at - 1))

    level = one(*cuts[0])
    for cut in cuts[1:]:
        level = level * one(*cut)
    return level


def deal_out(own_key, own, number, rows, count, top, limit, slope):
    order = jax.random.permutation(own_key, count)
    crowded, common = shares(count, rows * top, limit, slope, True), shares(count, rows * top, limit, slope, False)
    places = jnp.arange(count)

    def named(sizes, offset_by):
        used = int((sizes > 0).sum())
        fixed = max(1, used // 4)
        passed = fixed + (places - fixed + offset_by * (used - fixed)) % max(1, count - fixed)
        return jnp.zeros((count,), jnp.int32).at[order[jnp.where(places < fixed, places, passed)]].set(jnp.asarray(sizes, jnp.int32))

    sizes = jnp.where(number % 4 == 0, named(crowded, number // 4), named(common, number - number // 4 - 1))
    mixed = jax.random.permutation(jax.random.fold_in(own, 3), count)
    giver, taker = mixed[0:count // 2 * 2:2], mixed[1:count // 2 * 2:2]
    room = jnp.minimum(sizes[giver] - 1, limit - sizes[taker]) // 2
    room = jnp.where((giver == order[0]) | (taker == order[0]) | (sizes[taker] == 0), 0, jnp.maximum(room, 0))
    passed = jax.random.randint(jax.random.fold_in(own, 4), (count // 2,), 0, 1 << 20) % (room + 1)
    sizes = sizes.at[giver].add(-passed).at[taker].add(passed)
    members = jnp.searchsorted(jnp.cumsum(sizes), jnp.arange(rows * top), side="right").astype(jnp.int32)
    table = members.reshape(top, rows).T
    table = table[jax.random.permutation(jax.random.fold_in(own, 1), rows)]
    offset_by = jax.random.randint(jax.random.fold_in(own, 2), (rows, 1), 0, top)
    return jnp.take_along_axis(table, (jnp.arange(top)[None, :] + offset_by) % top, axis=1)


def shares(number_of, total, limit, slope, full):
    loads = [(1 << 20) // math.isqrt(grade ** slope) + 1 for grade in range(1, number_of + 1)]
    largest = limit if full else min(limit, max(-(-total // number_of), total * loads[0] // sum(loads)))
    least = 1 if total - largest >= number_of - 1 else 0
    given, surplus = [largest] + [least] * (number_of - 1), total - largest - least * (number_of - 1)
    while surplus > 0:
        candidates = [i for i in range(1, number_of) if given[i] < largest] or [i for i in range(1, number_of) if given[i] < limit]
        pool, budget = sum([loads[i] for i in candidates]), surplus
        for i in candidates:
            addition = min(limit - given[i], max(1, budget * loads[i] // pool), surplus)
            given[i] = given[i] + addition
            surplus = surplus - addition
    return np.array(given)


def centred(stream_key, dims, spread, reach, cuts=(), kind=jnp.bfloat16):
    entries = jax.random.normal(stream_key, dims, jnp.float32) * spread
    if len(cuts) > 0:
        entries = shard_levels(stream_key, dims, cuts, -0.22, 0.18) * entries
    return jnp.clip(entries, min=-reach, max=reach).astype(kind)


def setup_inputs(seed: int = 0) -> dict:
    arg_keys = jax.random.split(jax.random.key(seed), 11)
    query_rows = draw_query_rows(jax.random.fold_in(arg_keys[10], 71), 0)
    key_rows = draw_key_rows(jax.random.fold_in(arg_keys[10], 71), 0)
    value_rows = centred(arg_keys[2], (SEQS, LENGTH, KV_HEADS * HEAD), 1.0, 6.0, ((0, 32), (1, 8)))
    residual = centred(arg_keys[3], (SEQS, LENGTH, D), 1.0, 6.0, ((0, 32), (2, 8)))
    out_weight = centred(arg_keys[4], (HEADS * HEAD, D), (HEADS * HEAD) ** -0.5, 0.125, ((1, 8),))
    norm_gain = jnp.clip(1.0 + 0.15 * jax.random.normal(arg_keys[5], (D,), jnp.float32), 0.25, 1.75)
    gate_up = centred(arg_keys[6], (2 * EXPERTS, D, FF), D ** -0.5, 0.125, ((0, 256),))
    down_proj = centred(arg_keys[7], (2 * EXPERTS, HALF, D), FF ** -0.5, 0.21875, ((0, 256),))
    expert_ids_keys = jax.random.split(jax.random.fold_in(arg_keys[8], 1), SEQS * LENGTH // LENGTH)
    expert_ids_turns = jax.random.permutation(jax.random.fold_in(arg_keys[8], 3), SEQS * LENGTH // LENGTH)
    expert_ids = jax.vmap(lambda own, number: deal_out(jax.random.fold_in(arg_keys[8], 2), own, number, LENGTH, EXPERTS, TOP, CAP, 2))(expert_ids_keys, expert_ids_turns).reshape((SEQS, LENGTH, TOP))
    gate_vals = jnp.clip(jnp.exp(math.log(0.3) - 2.7080503 * jax.random.uniform(arg_keys[9], (SEQS, LENGTH, TOP), jnp.float32) ** shard_levels(arg_keys[9], (SEQS, LENGTH, TOP), ((0, 32),), -0.2, 0.2)), 0.02, 0.3)
    return {"query_rows": query_rows, "key_rows": key_rows, "value_rows": value_rows, "residual": residual, "out_weight": out_weight, "norm_gain": norm_gain, "gate_up": gate_up, "down_proj": down_proj, "expert_ids": expert_ids, "gate_vals": gate_vals}


neg_large = -1e+30
norm_eps = 1e-06

def attend(query_seq, key_seq, value_seq):
    grouped_q = query_seq.astype(jnp.float32).reshape(LENGTH, KV_HEADS, HEADS // KV_HEADS, HEAD)
    grouped_k = key_seq.astype(jnp.float32).reshape(LENGTH, KV_HEADS, HEAD)
    grouped_v = value_seq.astype(jnp.float32).reshape(LENGTH, KV_HEADS, HEAD)
    scores = jnp.einsum('qkgd,tkd->qkgt', grouped_q, grouped_k) * HEAD ** (-0.5)
    position = jnp.arange(LENGTH, dtype=jnp.int32)
    allowed = (position[None, :] <= position[:, None])[:, None, None, :]
    scores = jnp.where(allowed, scores, neg_large)
    row_max = lax.optimization_barrier(jnp.max(scores, axis=-1))
    exps = jnp.where(allowed, jnp.exp(scores - row_max[..., None]), 0.0)
    totals = lax.optimization_barrier(jnp.sum(exps, axis=-1))
    probs = lax.optimization_barrier(exps.astype(jnp.bfloat16)).astype(jnp.float32)
    mixed = jnp.einsum('qkgt,tkd->qkgd', probs, grouped_v) / totals[..., None]
    return mixed.reshape(LENGTH, HEADS * HEAD).astype(jnp.bfloat16)

def reference(query_rows, key_rows, value_rows, residual, out_weight, norm_gain, gate_up, down_proj, expert_ids, gate_vals):

    def expert_pair(pack):
        expert_index, rows = pack
        my_class = expert_index // GROUP
        owner = expert_index % GROUP
        results = []
        for half_index in range(2):
            block = (2 * my_class + half_index) * GROUP + owner
            projected = jnp.dot(rows, gate_up[block], preferred_element_type=jnp.float32)
            hidden_units = (jax.nn.silu(projected[:, :HALF]) * projected[:, HALF:]).astype(jnp.bfloat16)
            results.append(jnp.dot(hidden_units, down_proj[block], preferred_element_type=jnp.float32).astype(jnp.bfloat16))
        return jnp.stack(results)

    def class_sum(data_rows, token_ids):
        return jax.ops.segment_sum(data_rows, token_ids, num_segments=LENGTH + 1)[:LENGTH]

    def class_halves(data_pair, token_ids):
        return jax.vmap(class_sum, in_axes=(0, None))(data_pair, token_ids)

    def one_sequence(pack):
        query_seq, key_seq, value_seq, resid_seq, ids_seq, gates_seq = pack
        context = attend(query_seq, key_seq, value_seq)
        hidden_state = resid_seq.astype(jnp.float32) + jnp.dot(context, out_weight, preferred_element_type=jnp.float32)
        inv_rms = lax.rsqrt(lax.optimization_barrier(jnp.mean(hidden_state * hidden_state, axis=1)) + norm_eps)
        normed = (hidden_state * inv_rms[:, None] * norm_gain[None, :]).astype(jnp.bfloat16)
        flat_ids = ids_seq.reshape(-1)
        flat_gates = gates_seq.reshape(-1)
        pair_token = jnp.arange(LENGTH * TOP, dtype=jnp.int32) // TOP
        onehot = (flat_ids[:, None] == jnp.arange(EXPERTS, dtype=jnp.int32)[None, :]).astype(jnp.int32)
        ranks = lax.optimization_barrier(jnp.sum(jnp.cumsum(onehot, axis=0) * onehot, axis=1)) - 1
        token_table = jnp.full((EXPERTS, CAP), LENGTH, jnp.int32).at[flat_ids, ranks].set(pair_token, mode='drop')
        gate_table = jnp.zeros((EXPERTS, CAP), jnp.float32).at[flat_ids, ranks].set(flat_gates, mode='drop')
        padded = jnp.concatenate([normed, jnp.zeros((1, D), jnp.bfloat16)], axis=0)
        rows = padded[token_table]
        outputs = lax.map(expert_pair, (jnp.arange(EXPERTS, dtype=jnp.int32), rows))
        weighted = lax.optimization_barrier(outputs).astype(jnp.float32) * gate_table[:, None, :, None]
        grouped = weighted.reshape(CLASSES, GROUP, 2, CAP, D).transpose(0, 2, 1, 3, 4).reshape(CLASSES, 2, GROUP * CAP, D)
        tokens_grouped = token_table.reshape(CLASSES, GROUP * CAP)
        partials = jax.vmap(class_halves)(grouped, tokens_grouped)
        rounded = lax.optimization_barrier(partials.astype(jnp.bfloat16)).astype(jnp.float32)
        moe_sum = lax.optimization_barrier(jnp.sum(rounded, axis=(0, 1)))
        return (hidden_state + moe_sum).astype(jnp.bfloat16)
    return lax.map(one_sequence, (query_rows, key_rows, value_rows, residual, expert_ids, gate_vals))
```

```python
import jax
import jax.numpy as jnp
from jax import lax
from jax.experimental import pallas as pl
from jax.experimental.pallas import tpu as pltpu
from jax.sharding import PartitionSpec as P

LENGTH = 1024
D = 2048
HEAD = 128
TOP = 8
SLOTS = 80
BLK = 256
MESH = pl.DeviceIdType.MESH
norm_eps = 1e-06


def whole(
    q_ref, k_ref, v_ref, res_ref, w_ref, gain_ref, ids_ref, gates_ref, gu_ref, dp_ref,
    out_ref,
    kvb, cb, idb, gtb, rank, gate, tab, xb, sb, rb, gw, dw, hid, sq, ctt, rsend, rrecv,
    s_kv, r_kv, s_cx, r_cx, s_id, r_id, s_sq, r_sq, s_w, r_w, l_w, s_c, r_c2,
    s_z, r_z, s_f, r_f, s_o, r_o, s_r, r_r,
):
    ctx = lax.axis_index("ctx")
    exp = lax.axis_index("exp")
    z_hi, y = ctx // 4, ctx % 4
    z_lo, j = exp // 8, exp % 8
    x, core = j // 2, j % 2
    z = z_hi * 4 + z_lo
    mirror = (z_hi + 1) % 2 * 4 + y

    def at_z(to):
        return ((to // 4) * 4 + y, (to % 4) * 8 + j)

    def remote(src, dst, send, recv, where):
        return pltpu.make_async_remote_copy(
            src_ref=src, dst_ref=dst, send_sem=send, recv_sem=recv,
            device_id=where, device_id_type=MESH,
        )

    def bytes_of(ref, sem):
        return pltpu.make_async_copy(ref, ref, sem)

    barrier = pltpu.get_barrier_semaphore()

    def greet(where):
        pl.semaphore_signal(barrier, inc=1, device_id=where, device_id_type=MESH)

    @pl.loop(0, 32)
    def _(n):
        yy, jj = n // 8, n % 8

        @pl.when(jnp.logical_or(yy != y, jj != j))
        def _():
            greet((z_hi * 4 + yy, z_lo * 8 + jj))

    @pl.loop(1, 8)
    def _(n):
        greet(at_z((z + n) % 8))

    @pl.loop(1, 4)
    def _(n):
        greet(((z_hi + 1) % 2 * 4 + (y + n) % 4, exp))

    pl.semaphore_wait(barrier, 31 + 7 + 3)

    def id_copies(n):
        to = (ctx, (z_lo + n) % 4 * 8 + j)
        return (
            remote(ids_ref, idb.at[z_lo], s_id.at[0, n], r_id.at[0, z_lo], to),
            remote(gates_ref, gtb.at[z_lo], s_id.at[1, n], r_id.at[1, z_lo], to),
        )

    own = pl.ds(pl.multiple_of(ctx * 128, 128), 128)
    kvb[0, own, :] = k_ref[...]
    kvb[1, own, :] = v_ref[...]

    def kv_copy(slot, n, sem):
        rows = pl.ds(pl.multiple_of(slot * 128, 128), 128)
        part = kvb.at[:, rows, :]
        return remote(part, part, s_kv.at[sem], r_kv.at[slot], (z_hi * 4 + (y + n) % 4, exp))

    def kv_over():
        part = kvb.at[:, own, :]
        return remote(part, part, s_kv.at[0], r_kv.at[ctx], (mirror, exp))

    @pl.when(z_hi == 0)
    def _():
        kv_over().start()
        kvb[:, 512:1024, :] = jnp.zeros((2, 512, 256), jnp.bfloat16)

    for n in (1, 2, 3):
        kv_copy(ctx, n, n).start()
    for n in (1, 2, 3):
        for copy in id_copies(n):
            copy.start()
    idb[z_lo] = ids_ref[...]
    gtb[z_lo] = gates_ref[...]

    mine = core == y % 2
    sibling = (ctx, exp + 1 - 2 * core)
    across = (ctx + 1 - 2 * (y % 2), exp)

    def own_local():
        return (
            pltpu.make_async_copy(gu_ref, gw.at[0], l_w.at[0]),
            pltpu.make_async_copy(dp_ref, dw.at[0], l_w.at[1]),
        )

    def own_sibling():
        return (
            remote(gu_ref, gw.at[0], s_w.at[0], r_w.at[0], sibling),
            remote(dp_ref, dw.at[0], s_w.at[1], r_w.at[1], sibling),
        )

    def own_across():
        return (
            remote(gu_ref, gw.at[1], s_w.at[0], r_w.at[2], across),
            remote(dp_ref, dw.at[1], s_w.at[1], r_w.at[3], across),
        )

    def pass_sibling():
        return (
            remote(gw.at[1], gw.at[1], s_c.at[0], r_c2.at[0], sibling),
            remote(dw.at[1], dw.at[1], s_c.at[1], r_c2.at[1], sibling),
        )

    @pl.when(mine)
    def _():
        for copy in own_local() + own_sibling():
            copy.start()

    @pl.when(jnp.logical_not(mine))
    def _():
        for copy in own_across():
            copy.start()

    rrecv[0, 0, 128:256, :] = jnp.zeros((128, LENGTH), jnp.bfloat16)
    rrecv[1, 0, 0:128, :] = jnp.zeros((128, LENGTH), jnp.bfloat16)

    for n in (1, 2, 3):
        at = (z_lo + n) % 4
        bytes_of(idb.at[at], r_id.at[0, at]).wait()
        bytes_of(gtb.at[at], r_id.at[1, at]).wait()

    @pl.loop(0, 4)
    def _(s):
        number = lax.broadcasted_iota(jnp.int32, (16, LENGTH), 0)
        number = z_hi * 64 + z_lo * 8 + jnp.where(number >= 8, number + 24, number)
        found = jnp.zeros((16, LENGTH), jnp.float32)
        weight = jnp.zeros((16, LENGTH), jnp.float32)
        ids, gates = idb[s], gtb[s]
        for k in range(TOP):
            same = ids[k : k + 1, :] == number
            found = found + jnp.where(same, 1.0, 0.0)
            weight = weight + jnp.where(same, gates[k : k + 1, :], 0.0)
        rows = pl.ds(pl.multiple_of(s * 16, 16), 16)
        rank[rows, :] = found
        gate[rows, :] = weight

    members = rank[...]
    members16 = members.astype(jnp.bfloat16)
    before = []
    for b in range(8):
        row = lax.broadcasted_iota(jnp.int32, (LENGTH, 128), 0)
        column = lax.broadcasted_iota(jnp.int32, (LENGTH, 128), 1) + b * 128
        earlier = jnp.where(row < column, 1.0, 0.0).astype(jnp.bfloat16)
        before.append(jnp.dot(members16, earlier, preferred_element_type=jnp.float32))
    rank[...] = jnp.where(members > 0.5, jnp.concatenate(before, axis=1), -1.0)

    place = lambda: lax.broadcasted_iota(jnp.int32, (SLOTS, LENGTH), 0).astype(jnp.float32)

    @pl.loop(0, 64)
    def _(n):
        row = rank[pl.ds(n, 1), :]
        tab[n] = jnp.where(row == place(), 1.0, 0.0).astype(jnp.bfloat16)

    @pl.when(z_hi == 1)
    def _():
        bytes_of(kvb.at[:, pl.ds(0, 128), :], r_kv.at[mirror]).wait()
        for n in (1, 2, 3):
            kv_copy(mirror, n, 3 + n).start()

    for n in (1, 2, 3):
        bytes_of(kvb.at[:, pl.ds(0, 128), :], r_kv.at[z_hi * 4 + (y + n) % 4]).wait()

    @pl.when(z_hi == 1)
    def _():
        for n in (1, 2, 3):
            bytes_of(kvb.at[:, pl.ds(0, 128), :], r_kv.at[(y + n) % 4]).wait()

    def cx_part(g, slot):
        return cb.at[pl.ds(4 * g, 4), pl.ds(pl.multiple_of(slot * 128, 128), 128), :]

    def cx_copy(g, slot, n, sem):
        part = cx_part(g, slot)
        return remote(
            part, part, s_cx.at[g, sem], r_cx.at[g, slot], (z_hi * 4 + (y + n) % 4, exp)
        )

    def cx_over(g):
        part = cx_part(g, ctx)
        return remote(part, part, s_cx.at[g, 0], r_cx.at[g, ctx], (mirror, exp))

    def cx_wait(g, slot):
        bytes_of(cx_part(g, slot), r_cx.at[g, slot]).wait()

    for g in range(2):
        lanes = slice(g * 128, g * 128 + 128)

        @pl.loop(0, 4)
        def _(n):
            results = []
            for i in range(2):
                cols = pl.ds(pl.multiple_of((g * 8 + n * 2 + i) * 128, 128), 128)
                scores = lax.dot_general(
                    q_ref[:, cols], kvb[0, :, lanes], (((1,), (1,)), ((), ())),
                    preferred_element_type=jnp.float32,
                ) * (HEAD**-0.5)
                row = lax.broadcasted_iota(jnp.int32, (128, LENGTH), 0) + ctx * 128
                column = lax.broadcasted_iota(jnp.int32, (128, LENGTH), 1)
                scores = jnp.where(column <= row, scores, -1e30)
                top = jnp.max(scores, axis=1, keepdims=True)
                weights = jnp.exp(scores - top)
                total = jnp.sum(weights, axis=1, keepdims=True)
                mixed = jnp.dot(
                    weights.astype(jnp.bfloat16), kvb[1, :, lanes],
                    preferred_element_type=jnp.float32,
                )
                results.append((mixed / total).astype(jnp.bfloat16))
            cb[g * 4 + n, own, :] = jnp.concatenate(results, axis=1)

        cx_over(g).start()
        for n in (1, 2, 3):
            cx_copy(g, ctx, n, n).start()

    for g in range(2):
        cx_wait(g, mirror)
        for n in (1, 2, 3):
            cx_copy(g, mirror, n, 3 + n).start()
    for g in range(2):
        for n in (1, 2, 3):
            cx_wait(g, z_hi * 4 + (y + n) % 4)
    for g in range(2):
        for n in (1, 2, 3):
            cx_wait(g, (z_hi + 1) % 2 * 4 + (y + n) % 4)

    for b in range(4):
        rows = slice(b * 256, b * 256 + 256)
        total = res_ref[rows, :].astype(jnp.float32)
        for f in range(8):
            total = total + jnp.dot(
                cb[f, rows, :], w_ref[f * BLK : f * BLK + BLK, :],
                preferred_element_type=jnp.float32,
            )
        hid[rows, :] = total
        squares = total * total
        squares = squares[:, :128] + squares[:, 128:]
        sq[ctx, :, rows] = jnp.sum(squares.T, axis=0, keepdims=True)

    def sq_copy(n):
        to = (ctx + n) % 8
        return remote(sq.at[ctx], sq.at[ctx], s_sq.at[n], r_sq.at[ctx], (to, exp))

    for n in range(1, 8):
        sq_copy(n).start()
    for n in range(1, 8):
        at = (ctx + n) % 8
        bytes_of(sq.at[at], r_sq.at[at]).wait()
    total = sq[0]
    for n in range(1, 8):
        total = total + sq[n]
    inverse = lax.rsqrt(total / D + norm_eps)
    for b in range(4):
        rows = slice(b * 256, b * 256 + 256)
        column = jnp.broadcast_to(inverse[:, rows], (128, 256)).T
        column = jnp.concatenate([column, column], axis=1)
        xb[z, rows, :] = (hid[rows, :] * column * gain_ref[...]).astype(jnp.bfloat16)

    right, left = at_z((z + 1) % 8), at_z((z + 7) % 8)

    def z_right(i):
        part = xb.at[(z + 8 - i) % 8]
        if i == 3:
            part = part.at[0:512]
        return remote(part, part, s_z.at[0, i], r_z.at[0, i], right)

    def z_left(i):
        part = xb.at[(z + i) % 8]
        if i == 3:
            part = part.at[512:1024]
        return remote(part, part, s_z.at[1, i], r_z.at[1, i], left)

    def is_me(s, yy, xx):
        return jnp.logical_and(s % 2 == core, jnp.logical_and(yy == y, xx == x))

    def deal(zz):
        s, half = zz % 4, zz // 4
        col = pl.ds(pl.multiple_of((half * 4 + y) * BLK, BLK), BLK)
        to_rows = pl.ds(pl.multiple_of((s // 2 * 8 + j) * SLOTS, SLOTS), SLOTS)
        dst = rb.at[to_rows, col]

        @pl.loop(0, 4)
        def _(n):
            lhs = tab[pl.ds(s * 16 + n * 4, 4)].reshape(4 * SLOTS, LENGTH)
            rows = pl.ds(pl.multiple_of(n * 4 * SLOTS, 4 * SLOTS), 4 * SLOTS)
            sb[zz, rows, :] = jnp.dot(
                lhs, xb[zz], preferred_element_type=jnp.float32
            ).astype(jnp.bfloat16)

            @pl.loop(0, 4)
            def _(i):
                e = n * 4 + i
                yy, xx = e // 8 * 2 + e % 2, e % 8 // 2
                src = sb.at[zz, pl.ds(pl.multiple_of(e * SLOTS, SLOTS), SLOTS), :]
                same = is_me(s, yy, xx)

                @pl.when(same)
                def _():
                    pltpu.make_async_copy(src, dst, r_f.at[s // 2]).start()

                @pl.when(jnp.logical_not(same))
                def _():
                    to = (z_hi * 4 + yy, z_lo * 8 + xx * 2 + s % 2)
                    remote(src, dst, s_f.at[zz], r_f.at[s // 2], to).start()

    z_right(0).start()
    z_left(0).start()
    for g in range(2):
        cx_over(g).wait_send()
        for n in (1, 2, 3):
            cx_copy(g, ctx, n, n).wait_send()
            cx_copy(g, mirror, n, 3 + n).wait_send()
    deal(z)
    for i in range(3):
        z_right(i).wait_recv()
        z_right(i + 1).start()
        z_left(i).wait_recv()
        z_left(i + 1).start()
        deal((z + 7 - i) % 8)
        deal((z + 1 + i) % 8)
        if i == 1:

            @pl.when(mine)
            def _():
                for n in (0, 1):
                    bytes_of((gw, dw)[n].at[1], r_w.at[2 + n]).wait()
                for copy in pass_sibling():
                    copy.start()

    z_right(3).wait_recv()
    z_left(3).wait_recv()
    deal((z + 4) % 8)

    @pl.when(mine)
    def _():
        for copy in own_local():
            copy.wait()

    @pl.when(jnp.logical_not(mine))
    def _():
        for n in (0, 1):
            bytes_of((gw, dw)[n].at[0], r_w.at[n]).wait()
            bytes_of((gw, dw)[n].at[1], r_c2.at[n]).wait()

    @pl.loop(0, 8)
    def _(zz):
        some = (zz % 4) % 2 == core

        @pl.when(some)
        def _():
            bytes_of(sb.at[zz, 0 : 15 * SLOTS], s_f.at[zz]).wait()

        @pl.when(jnp.logical_not(some))
        def _():
            bytes_of(sb.at[zz], s_f.at[zz]).wait()

    def distance(zz):
        up = (zz + 8 - z) % 8
        return jnp.minimum(up, 8 - up)

    my_e = y // 2 * 8 + x * 2 + y % 2

    for p in range(2):
        bytes_of(rb.at[p * 640 : p * 640 + 640], r_f.at[p]).wait()

    for turn in range(2):
        p = (z_lo // 2 + turn) % 2
        s = 2 * p + core

        @pl.loop(0, 2)
        def _(n):
            rows = pl.ds(pl.multiple_of(p * 640 + n * 320, 320), 320)
            units = []
            for h in range(2):
                u = jnp.dot(rb[rows, :], gw[h], preferred_element_type=jnp.float32)
                v = u[:, :384]
                units.append((v / (1.0 + jnp.exp(-v)) * u[:, 384:]).astype(jnp.bfloat16))
            for f in range(8):
                cols = slice(f * BLK, f * BLK + BLK)
                sb[f, rows, :] = (
                    jnp.dot(units[0], dw[0, :, cols], preferred_element_type=jnp.float32)
                    + jnp.dot(units[1], dw[1, :, cols], preferred_element_type=jnp.float32)
                ).astype(jnp.bfloat16)

        first = jnp.where(distance(s) >= distance(4 + s), 0, 1)

        @pl.loop(0, 2)
        def _(m):
            half = (first + m) % 2
            slot = half * 4 + s
            dst = cb.at[slot, pl.ds(pl.multiple_of(my_e * SLOTS, SLOTS), SLOTS), :]

            @pl.loop(0, 32)
            def _(n):
                yy, jj = n % 4, n // 4
                from_rows = pl.ds(pl.multiple_of((p * 8 + jj) * SLOTS, SLOTS), SLOTS)
                src = sb.at[half * 4 + yy, from_rows, :]
                same = jnp.logical_and(yy == y, jj == j)

                @pl.when(same)
                def _():
                    pltpu.make_async_copy(src, dst, r_o.at[slot]).start()

                @pl.when(jnp.logical_not(same))
                def _():
                    to = (z_hi * 4 + yy, z_lo * 8 + jj)
                    remote(src, dst, s_o.at[p, half], r_o.at[slot], to).start()

    @pl.loop(0, 64)
    def _(n):
        row = rank[pl.ds(n, 1), :]
        tab[n] = jnp.where(row == place(), gate[pl.ds(n, 1), :], 0.0).astype(jnp.bfloat16)

    def turned(zz):
        bytes_of(cb.at[zz], r_o.at[zz]).wait()
        ctt[...] = cb[zz].T

    def tile(zz, t):
        rhs = tab[pl.ds(zz % 4 * 16, 16), :, t].reshape(16 * SLOTS, 256)
        return jnp.dot(ctt[...], rhs, preferred_element_type=jnp.float32)

    def tiles(body):
        @pl.loop(0, 4)
        def _(n):
            body(pl.ds(pl.multiple_of(n * 256, 256), 256))

    def r_copy(way, i):
        to = (right, left)[way]
        if i == 0:
            rows = slice(0, 128) if way == 0 else slice(128, 256)
            src, dst = rsend.at[0, 0, rows], rrecv.at[way, 0, rows]
        else:
            src, dst = rsend.at[way, i], rrecv.at[way, i]
        return remote(src, dst, s_r.at[way, i], r_r.at[way, i], to)

    far = (z + 4) % 8
    turned(far)

    def start_far(t):
        rsend[0, 0, :, t] = tile(far, t).astype(jnp.bfloat16)

    tiles(start_far)
    r_copy(0, 0).start()
    r_copy(1, 0).start()
    for i in range(1, 4):
        for way in range(2):
            zz = (z + 4 - i) % 8 if way == 0 else (z + 4 + i) % 8
            turned(zz)
            r_copy(way, i - 1).wait_recv()

            def add(t, zz=zz, way=way, i=i):
                rsend[way, i, :, t] = (
                    tile(zz, t) + rrecv[way, i - 1, :, t].astype(jnp.float32)
                ).astype(jnp.bfloat16)

            tiles(add)
            r_copy(way, i).start()
    turned(z)
    r_copy(0, 3).wait_recv()
    r_copy(1, 3).wait_recv()

    def finish(t):
        total = (
            tile(z, t)
            + rrecv[0, 3, :, t].astype(jnp.float32)
            + rrecv[1, 3, :, t].astype(jnp.float32)
        )
        out_ref[t, :] = (hid[t, :] + total.T).astype(jnp.bfloat16)

    tiles(finish)

    @pl.when(z_hi == 0)
    def _():
        kv_over().wait_send()

    @pl.when(z_hi == 1)
    def _():
        for n in (1, 2, 3):
            kv_copy(mirror, n, 3 + n).wait_send()

    for n in (1, 2, 3):
        kv_copy(ctx, n, n).wait_send()
        for copy in id_copies(n):
            copy.wait_send()
    for n in range(1, 8):
        sq_copy(n).wait_send()

    @pl.when(mine)
    def _():
        for copy in own_sibling():
            copy.wait_send()

    @pl.when(mine)
    def _():
        for copy in pass_sibling():
            copy.wait_send()

    @pl.when(jnp.logical_not(mine))
    def _():
        for copy in own_across():
            copy.wait_send()

    for i in range(4):
        z_right(i).wait_send()
        z_left(i).wait_send()
        r_copy(0, i).wait_send()
        r_copy(1, i).wait_send()
    for p in range(2):
        for half in range(2):
            bytes_of(sb.at[0:5, 0:496], s_o.at[p, half]).wait()


def shards(q, k, v, residual, w, gain, gate_up, down, ids, gates):
    vmem = pl.BlockSpec(memory_space=pltpu.VMEM)
    anywhere = pl.BlockSpec(memory_space=pl.ANY)
    bf16, f32 = jnp.bfloat16, jnp.float32
    dma = pltpu.SemaphoreType.DMA
    out = pl.pallas_call(
        whole,
        out_shape=jax.ShapeDtypeStruct((LENGTH, BLK), bf16),
        in_specs=[vmem] * 8 + [anywhere] * 2,
        out_specs=vmem,
        scratch_shapes=[
            pltpu.VMEM((2, LENGTH, 256), bf16),
            pltpu.VMEM((8, 16 * SLOTS, BLK), bf16),
            pltpu.VMEM((4, TOP, LENGTH), jnp.int32),
            pltpu.VMEM((4, TOP, LENGTH), f32),
            pltpu.VMEM((64, LENGTH), f32),
            pltpu.VMEM((64, LENGTH), f32),
            pltpu.VMEM((64, SLOTS, LENGTH), bf16),
            pltpu.VMEM((8, LENGTH, BLK), bf16),
            pltpu.VMEM((8, 16 * SLOTS, BLK), bf16),
            pltpu.VMEM((16 * SLOTS, D), bf16),
            pltpu.VMEM((2, D, 768), bf16),
            pltpu.VMEM((2, 384, D), bf16),
            pltpu.VMEM((LENGTH, BLK), f32),
            pltpu.VMEM((8, 1, LENGTH), f32),
            pltpu.VMEM((BLK, 16 * SLOTS), bf16),
            pltpu.VMEM((2, 4, BLK, LENGTH), bf16),
            pltpu.VMEM((2, 4, BLK, LENGTH), bf16),
            dma((8,)), dma((8,)), dma((2, 8)), dma((2, 8)), dma((2, 4)), dma((2, 4)),
            dma((8,)), dma((8,)), dma((2,)), dma((4,)), dma((2,)), dma((2,)), dma((2,)),
            dma((2, 4)), dma((2, 4)), dma((8,)), dma((2,)), dma((2, 2)), dma((8,)),
            dma((2, 4)), dma((2, 4)),
        ],
        compiler_params=pltpu.CompilerParams(
            collective_id=0, has_side_effects=True, vmem_limit_bytes=63 * 1024 * 1024
        ),
    )(
        q[0], k[0], v[0], residual[0], w, gain[None], ids[0].T, gates[0].T,
        gate_up[0], down[0],
    )
    return out[None]


def solution(mesh):
    return jax.shard_map(
        shards,
        mesh=mesh,
        in_specs=(
            P("exp", "ctx", None),
            P("exp", "ctx", None),
            P("exp", "ctx", None),
            P("exp", None, "ctx"),
            P(None, "ctx"),
            P("ctx"),
            P(("ctx", "exp"), None, None),
            P(("ctx", "exp"), None, None),
            P("exp", None, None),
            P("exp", None, None),
        ),
        out_specs=P("exp", None, "ctx"),
        check_vma=False,
    )
```

```python
import jax
import jax.numpy as jnp
from jax import lax
from jax.experimental import pallas as pl
from jax.experimental.pallas import tpu as pltpu
from jax.sharding import PartitionSpec as P

LENGTH = 1024
D = 2048
HEAD = 128
TOP = 8
SLOTS = 80
BLK = 256
MESH = pl.DeviceIdType.MESH
norm_eps = 1e-06


def whole(
    q_ref, k_ref, v_ref, res_ref, w_ref, gain_ref, ids_ref, gates_ref, gu_ref, dp_ref,
    out_ref,
    kvb, cb, idb, gtb, rank, gate, tab, xb, sb, rb, gw, dw, hid, sq, ctt, rsend, rrecv, wm, resm, gm, hs, hm, acc, base,
    s_kv, r_kv, s_cx, r_cx, s_wm, r_wm, s_rm, r_rm, s_id, r_id, s_sq, r_sq, s_w, r_w, l_w, s_c, r_c2,
    s_z, r_z, s_f, r_f, s_o, r_o, s_r, r_r,
):
    ctx = lax.axis_index("ctx")
    exp = lax.axis_index("exp")
    z_hi, y = ctx // 4, ctx % 4
    z_lo, j = exp // 8, exp % 8
    x, core = j // 2, j % 2
    z = z_hi * 4 + z_lo
    mirror = (z_hi + 1) % 2 * 4 + y

    def at_z(to):
        return ((to // 4) * 4 + y, (to % 4) * 8 + j)

    def remote(src, dst, send, recv, where):
        return pltpu.make_async_remote_copy(
            src_ref=src, dst_ref=dst, send_sem=send, recv_sem=recv,
            device_id=where, device_id_type=MESH,
        )

    def bytes_of(ref, sem):
        return pltpu.make_async_copy(ref, ref, sem)

    barrier = pltpu.get_barrier_semaphore()
    pending = []

    def greet(where):
        pl.semaphore_signal(barrier, inc=1, device_id=where, device_id_type=MESH)

    @pl.loop(0, 32)
    def _(n):
        yy, jj = n // 8, n % 8

        @pl.when(jnp.logical_or(yy != y, jj != j))
        def _():
            greet((z_hi * 4 + yy, z_lo * 8 + jj))

    @pl.loop(1, 8)
    def _(n):
        greet(at_z((z + n) % 8))

    pl.semaphore_wait(barrier, 31 + 7)

    def id_copies(n):
        to = (ctx, (z_lo + n) % 4 * 8 + j)
        return (
            remote(ids_ref, idb.at[z_lo], s_id.at[0, n], r_id.at[0, z_lo], to),
            remote(gates_ref, gtb.at[z_lo], s_id.at[1, n], r_id.at[1, z_lo], to),
        )

    own = pl.ds(pl.multiple_of(ctx * 128, 128), 128)
    kvb[0, own, :] = k_ref[...]
    kvb[1, own, :] = v_ref[...]

    def kv_copy(slot, n, sem):
        rows = pl.ds(pl.multiple_of(slot * 128, 128), 128)
        part = kvb.at[:, rows, :]
        return remote(part, part, s_kv.at[sem], r_kv.at[slot], (z_hi * 4 + (y + n) % 4, exp))

    def kv_over():
        part = kvb.at[:, own, :]
        return remote(part, part, s_kv.at[0], r_kv.at[ctx], (mirror, exp))

    @pl.when(z_hi == 0)
    def _():
        kv_over().start()
        kvb[:, 512:1024, :] = jnp.zeros((2, 512, 256), jnp.bfloat16)

    for n in (1, 2, 3):
        kv_copy(ctx, n, n).start()
    for n in (1, 2, 3):
        for copy in id_copies(n):
            copy.start()
    idb[z_lo] = ids_ref[...]
    gtb[z_lo] = gates_ref[...]

    def kv_sent():
        @pl.when(z_hi == 0)
        def _():
            kv_over().wait_send()

        for n in (1, 2, 3):
            kv_copy(ctx, n, n).wait_send()
            for copy in id_copies(n):
                copy.wait_send()

    pending.append(kv_sent)

    half_w = pl.ds(pl.multiple_of(core * 1024, 1024), 1024)
    here = pl.ds(pl.multiple_of(z_hi * 512, 512), 512)
    there = pl.ds(pl.multiple_of((1 - z_hi) * 512, 512), 512)
    other = (mirror, exp)

    def w_over(n):
        to = (mirror, jnp.where(z_lo == 3, n, 3 - n) * 8 + j)
        return remote(w_ref.at[half_w, :], wm.at[half_w, :], s_wm.at[n], r_wm.at[0], to)

    def w_sibling():
        return remote(
            wm.at[half_w, :], wm.at[half_w, :], s_wm.at[2], r_wm.at[1], (ctx, exp + 1 - 2 * core)
        )

    def res_over():
        return (
            remote(res_ref.at[there, :], resm, s_rm.at[0], r_rm.at[0], other),
            remote(gain_ref, gm, s_rm.at[1], r_rm.at[1], other),
        )

    @pl.when(jnp.logical_or(z_lo == 3, z_lo == 0))
    def _():
        w_over(0).start()
        w_over(1).start()

    def w_sent():
        @pl.when(jnp.logical_or(z_lo == 3, z_lo == 0))
        def _():
            w_over(0).wait_send()
            w_over(1).wait_send()

        w_sibling().wait_send()
        for copy in res_over():
            copy.wait_send()

    pending.append(w_sent)

    @pl.when(z_hi == 1)
    def _():
        for copy in res_over():
            copy.start()

    mine = core == y % 2
    sibling = (ctx, exp + 1 - 2 * core)
    across = (ctx + 1 - 2 * (y % 2), exp)

    def own_local():
        return (
            pltpu.make_async_copy(gu_ref, gw.at[0], l_w.at[0]),
            pltpu.make_async_copy(dp_ref, dw.at[0], l_w.at[1]),
        )

    def own_sibling():
        return (
            remote(gu_ref, gw.at[0], s_w.at[0], r_w.at[0], sibling),
            remote(dp_ref, dw.at[0], s_w.at[1], r_w.at[1], sibling),
        )

    cuts = (0, 1024, 1280, 2048)

    def own_across(n):
        if n == 3:
            return remote(dp_ref, dw.at[1], s_w.at[3], r_w.at[5], across)
        rows = slice(cuts[n], cuts[n + 1])
        return remote(gu_ref.at[rows], gw.at[1, rows], s_w.at[n], r_w.at[2 + n], across)

    def across_arrived():
        for n in range(3):
            bytes_of(gw.at[1, cuts[n] : cuts[n + 1]], r_w.at[2 + n]).wait()
        bytes_of(dw.at[1], r_w.at[5]).wait()

    def send_across(*which):
        @pl.when(jnp.logical_not(mine))
        def _():
            for n in which:
                own_across(n).start()

    def pass_sibling():
        return (
            remote(gw.at[1], gw.at[1], s_c.at[0], r_c2.at[0], sibling),
            remote(dw.at[1], dw.at[1], s_c.at[1], r_c2.at[1], sibling),
        )

    @pl.when(mine)
    def _():
        for copy in own_local() + own_sibling():
            copy.start()

    send_across(0)

    def weights_sent():
        @pl.when(mine)
        def _():
            for copy in own_sibling():
                copy.wait_send()

        @pl.when(jnp.logical_not(mine))
        def _():
            for n in range(4):
                own_across(n).wait_send()

    pending.append(weights_sent)

    rrecv[0, 0, 128:256, :] = jnp.zeros((128, LENGTH), jnp.bfloat16)
    rrecv[1, 0, 0:128, :] = jnp.zeros((128, LENGTH), jnp.bfloat16)

    for n in (1, 2, 3):
        at = (z_lo + n) % 4
        bytes_of(idb.at[at], r_id.at[0, at]).wait()
        bytes_of(gtb.at[at], r_id.at[1, at]).wait()

    @pl.loop(0, 4)
    def _(s):
        number = lax.broadcasted_iota(jnp.int32, (16, LENGTH), 0)
        number = z_hi * 64 + z_lo * 8 + jnp.where(number >= 8, number + 24, number)
        found = jnp.zeros((16, LENGTH), jnp.float32)
        weight = jnp.zeros((16, LENGTH), jnp.float32)
        ids, gates = idb[s], gtb[s]
        for k in range(TOP):
            same = ids[k : k + 1, :] == number
            found = found + jnp.where(same, 1.0, 0.0)
            weight = weight + jnp.where(same, gates[k : k + 1, :], 0.0)
        rows = pl.ds(pl.multiple_of(s * 16, 16), 16)
        rank[rows, :] = found
        gate[rows, :] = weight

    members = rank[...]
    members16 = members.astype(jnp.bfloat16)
    before = []
    for b in range(8):
        row = lax.broadcasted_iota(jnp.int32, (LENGTH, 128), 0)
        column = lax.broadcasted_iota(jnp.int32, (LENGTH, 128), 1) + b * 128
        earlier = jnp.where(row < column, 1.0, 0.0).astype(jnp.bfloat16)
        before.append(jnp.dot(members16, earlier, preferred_element_type=jnp.float32))
    rank[...] = jnp.where(members > 0.5, jnp.concatenate(before, axis=1), -1.0)

    place = lambda: lax.broadcasted_iota(jnp.int32, (SLOTS, LENGTH), 0).astype(jnp.float32)

    @pl.loop(0, 64)
    def _(n):
        row = rank[pl.ds(n, 1), :]
        tab[n] = jnp.where(row == place(), 1.0, 0.0).astype(jnp.bfloat16)

    @pl.when(z_hi == 1)
    def _():
        bytes_of(kvb.at[:, pl.ds(0, 128), :], r_kv.at[mirror]).wait()
        for n in (1, 2, 3):
            kv_copy(mirror, n, 3 + n).start()

    def kv_passed():
        @pl.when(z_hi == 1)
        def _():
            for n in (1, 2, 3):
                kv_copy(mirror, n, 3 + n).wait_send()

    pending.append(kv_passed)

    for n in (1, 2, 3):
        bytes_of(kvb.at[:, pl.ds(0, 128), :], r_kv.at[z_hi * 4 + (y + n) % 4]).wait()

    @pl.when(z_hi == 1)
    def _():
        for n in (1, 2, 3):
            bytes_of(kvb.at[:, pl.ds(0, 128), :], r_kv.at[(y + n) % 4]).wait()

    send_across(1)

    @pl.when(z_hi == 0)
    def _():
        for copy in res_over():
            copy.start()

    def cx_part(g, n, first=0, count=4):
        rows = pl.ds(pl.multiple_of((y + n) % 4 * 128, 128), 128)
        return cb.at[pl.ds(4 * g + first, count), rows, :]

    def cx_copy(g, way):
        if way < 2:
            part = cx_part(g, 0)
        elif way == 2:
            part = cx_part(g, 3, 0, 2)
        else:
            part = cx_part(g, 1, 2, 2)
        to = (z_hi * 4 + (y + (1 if way % 2 == 0 else 3)) % 4, exp)
        return remote(part, part, s_cx.at[g, way], r_cx.at[g, way], to)

    for g in range(2):
        lanes = slice(g * 128, g * 128 + 128)

        @pl.loop(0, 4)
        def _(n):
            results = []
            for i in range(2):
                cols = pl.ds(pl.multiple_of((g * 8 + n * 2 + i) * 128, 128), 128)
                scores = lax.dot_general(
                    q_ref[:, cols], kvb[0, :, lanes], (((1,), (1,)), ((), ())),
                    preferred_element_type=jnp.float32,
                ) * (HEAD**-0.5)
                row = lax.broadcasted_iota(jnp.int32, (128, LENGTH), 0) + ctx * 128
                column = lax.broadcasted_iota(jnp.int32, (128, LENGTH), 1)
                scores = jnp.where(column <= row, scores, -1e30)
                top = jnp.max(scores, axis=1, keepdims=True)
                weights = jnp.exp(scores - top)
                total = jnp.sum(weights, axis=1, keepdims=True)
                mixed = jnp.dot(
                    weights.astype(jnp.bfloat16), kvb[1, :, lanes],
                    preferred_element_type=jnp.float32,
                )
                results.append((mixed / total).astype(jnp.bfloat16))
            cb[g * 4 + n, pl.ds(pl.multiple_of(y * 128, 128), 128), :] = jnp.concatenate(results, axis=1)

        cx_copy(g, 0).start()
        cx_copy(g, 1).start()

    bytes_of(wm.at[half_w, :], r_wm.at[0]).wait()
    w_sibling().start()
    for g in range(2):
        for way in range(2):
            cx_copy(g, way).wait_recv()
            cx_copy(g, 2 + way).start()
    for g in range(2):
        for way in (2, 3):
            cx_copy(g, way).wait_recv()

    bytes_of(resm, r_rm.at[0]).wait()
    bytes_of(gm, r_rm.at[1]).wait()
    bytes_of(wm.at[half_w, :], r_wm.at[1]).wait()
    for b in range(2):
        rows = slice(b * 256, b * 256 + 256)
        mine_rows = pl.ds(pl.multiple_of(z_hi * 512 + b * 256, 256), 256)
        squares = jnp.zeros((256, 128), jnp.float32)
        for side, weight in enumerate((w_ref, wm)):
            total = (res_ref[mine_rows, :] if side == 0 else resm[rows, :]).astype(jnp.float32)
            for f in range(8):
                total = total + jnp.dot(
                    cb[f, rows, :], weight[f * BLK : f * BLK + BLK, :],
                    preferred_element_type=jnp.float32,
                )
            hid[side, rows, :] = total
            squared = total * total
            squares = squares + (squared[:, :128] + squared[:, 128:])
        sq[y, :, rows] = jnp.sum(squares.T, axis=0, keepdims=True)

    def sq_copy(n):
        to = (z_hi * 4 + (y + n) % 4, exp)
        return remote(sq.at[y], sq.at[y], s_sq.at[n], r_sq.at[y], to)

    for n in (1, 2, 3):
        sq_copy(n).start()
        pending.append(sq_copy(n).wait_send)
    send_across(2, 3)
    hs[...] = hid[1].astype(jnp.bfloat16)
    for n in (1, 2, 3):
        at = (y + n) % 4
        bytes_of(sq.at[at], r_sq.at[at]).wait()
    total = sq[0] + sq[1] + (sq[2] + sq[3])
    inverse = lax.rsqrt(total / D + norm_eps)
    for b in range(2):
        rows = slice(b * 256, b * 256 + 256)
        column = jnp.broadcast_to(inverse[:, rows], (128, 256)).T
        column = jnp.concatenate([column, column], axis=1)
        for side, gains in enumerate((gain_ref, gm)):
            xb[z_hi if side == 0 else 1 - z_hi, z, rows, :] = (
                hid[side, rows, :] * column * gains[...]
            ).astype(jnp.bfloat16)

    def hid_over():
        return remote(hs, hm, s_rm.at[2], r_rm.at[2], other)

    right, left = at_z((z + 1) % 8), at_z((z + 7) % 8)

    def z_copy(way, i, half):
        block = (z + 8 - i) % 8 if way == 0 else (z + i) % 8
        part = xb.at[half, block]
        if i == 3:
            part = part.at[0:256] if way == 0 else part.at[256:512]
        to = (right, left)[way]
        return remote(part, part, s_z.at[way, i, half], r_z.at[way, i, half], to)

    def is_me(s, yy, xx):
        return jnp.logical_and(s % 2 == core, jnp.logical_and(yy == y, xx == x))

    def deal(s, half):
        to_rows = pl.ds(pl.multiple_of((s // 2 * 8 + j) * SLOTS, SLOTS), SLOTS)
        dst = rb.at[to_rows, pl.ds(pl.multiple_of((half * 4 + y) * BLK, BLK), BLK)]
        zz = half * 4 + s

        @pl.loop(0, 4)
        def _(turn):
            n = (turn + y // 2 * 2 + x // 2) % 4
            lhs = tab[pl.ds(s * 16 + n * 4, 4)].reshape(4 * SLOTS, LENGTH)
            rows = pl.ds(pl.multiple_of(n * 4 * SLOTS, 4 * SLOTS), 4 * SLOTS)
            sb[zz, rows, :] = (
                jnp.dot(lhs[:, :512], xb[half, s], preferred_element_type=jnp.float32)
                + jnp.dot(lhs[:, 512:], xb[half, 4 + s], preferred_element_type=jnp.float32)
            ).astype(jnp.bfloat16)

            @pl.loop(0, 4)
            def _(i):
                e = n * 4 + (i + x % 2 * 2 + y % 2) % 4
                yy, xx = e // 8 * 2 + e % 2, e % 8 // 2
                src = sb.at[zz, pl.ds(pl.multiple_of(e * SLOTS, SLOTS), SLOTS), :]
                same = is_me(s, yy, xx)

                @pl.when(same)
                def _():
                    pltpu.make_async_copy(src, dst, r_f.at[s // 2]).start()

                @pl.when(jnp.logical_not(same))
                def _():
                    to = (z_hi * 4 + yy, z_lo * 8 + xx * 2 + s % 2)
                    remote(src, dst, s_f.at[zz], r_f.at[s // 2], to).start()

    for half in range(2):
        for way in range(2):
            z_copy(way, 0, half).start()
            pending += [z_copy(way, i, half).wait_send for i in range(4)]
    for g in range(2):
        for way in range(4):
            cx_copy(g, way).wait_send()
    for i in range(3):
        for half in range(2):
            for way in range(2):
                z_copy(way, i, half).wait_recv()
                z_copy(way, i + 1, half).start()
            if i == 1:
                deal((z_lo + 2) % 4, half)
            if i == 2:
                deal((z_lo + 1) % 4, half)
    for half in range(2):
        z_copy(0, 3, half).wait_recv()
        z_copy(1, 3, half).wait_recv()
        deal(z_lo, half)
    for half in range(2):
        deal((z_lo + 3) % 4, half)
    hid_over().start()
    pending.append(hid_over().wait_send)

    @pl.when(mine)
    def _():
        across_arrived()
        for copy in pass_sibling():
            copy.start()

    def weights_passed():
        @pl.when(mine)
        def _():
            for copy in pass_sibling():
                copy.wait_send()

    pending.append(weights_passed)
    @pl.when(mine)
    def _():
        for copy in own_local():
            copy.wait()

    @pl.when(jnp.logical_not(mine))
    def _():
        for n in (0, 1):
            bytes_of((gw, dw)[n].at[0], r_w.at[n]).wait()
            bytes_of((gw, dw)[n].at[1], r_c2.at[n]).wait()

    def dealt():
        @pl.loop(0, 8)
        def _(zz):
            some = (zz % 4) % 2 == core

            @pl.when(some)
            def _():
                bytes_of(sb.at[zz, 0 : 15 * SLOTS], s_f.at[zz]).wait()

            @pl.when(jnp.logical_not(some))
            def _():
                bytes_of(sb.at[zz], s_f.at[zz]).wait()

    pending.append(dealt)

    def distance(zz):
        up = (zz + 8 - z) % 8
        return jnp.minimum(up, 8 - up)

    my_e = y // 2 * 8 + x * 2 + y % 2

    def send_back(p, half, n):
        slot = half * 4 + 2 * p + core
        dst = cb.at[slot, pl.ds(pl.multiple_of(my_e * SLOTS, SLOTS), SLOTS), :]

        @pl.loop(0, 16)
        def _(m):
            yy, jj = (m + y) % 4, n * 4 + (m // 4 + x % 2 * 2 + core) % 4
            from_rows = pl.ds(pl.multiple_of((p * 8 + jj) * SLOTS, SLOTS), SLOTS)
            col = pl.ds(pl.multiple_of((half * 4 + yy) * BLK, BLK), BLK)
            src = rb.at[from_rows, col]
            same = jnp.logical_and(yy == y, jj == j)

            @pl.when(same)
            def _():
                pltpu.make_async_copy(src, dst, r_o.at[slot]).start()

            @pl.when(jnp.logical_not(same))
            def _():
                to = (z_hi * 4 + yy, z_lo * 8 + jj)
                remote(src, dst, s_o.at[p, half], r_o.at[slot], to).start()

    plain = core == z_lo % 2

    def far_half(p):
        s = 2 * p + core
        return jnp.where(distance(s) >= distance(4 + s), 0, 1)

    for turn in range(2):
        p = (z_lo // 2 + 1 + turn) % 2
        bytes_of(rb.at[pl.ds(pl.multiple_of(p * 640, 640), 640)], r_f.at[p]).wait()

        @pl.loop(0, 2)
        def _(m):
            n = (m + x // 2) % 2
            rows = pl.ds(pl.multiple_of(p * 640 + n * 320, 320), 320)
            units = []
            for h in range(2):
                u = jnp.dot(rb[rows, :], gw[h], preferred_element_type=jnp.float32)
                v = u[:, :384]
                units.append((v / (1.0 + jnp.exp(-v)) * u[:, 384:]).astype(jnp.bfloat16))

            def results(half):
                for i in range(4):
                    cols = pl.ds(pl.multiple_of((half * 4 + i) * BLK, BLK), BLK)
                    rb[rows, cols] = (
                        jnp.dot(units[0], dw[0, :, cols], preferred_element_type=jnp.float32)
                        + jnp.dot(units[1], dw[1, :, cols], preferred_element_type=jnp.float32)
                    ).astype(jnp.bfloat16)

            first = far_half(p)
            results(first)
            if turn == 1:
                send_back(p, first, n)
            else:

                @pl.when(jnp.logical_not(plain))
                def _():
                    send_back(p, first, n)

            results(1 - first)

    def send_both(p, half):
        @pl.loop(0, 2)
        def _(m):
            send_back(p, half, (m + x // 2) % 2)

    early, late = (z_lo // 2 + 1) % 2, z_lo // 2

    @pl.when(plain)
    def _():
        send_both(early, far_half(early))

    send_both(early, 1 - far_half(early))
    send_both(late, 1 - far_half(late))

    for p in range(2):
        for half in range(2):
            pending.append(bytes_of(sb.at[0:5, 0:496], s_o.at[p, half]).wait)

    @pl.loop(0, 64)
    def _(n):
        row = rank[pl.ds(n, 1), :]
        tab[n] = jnp.where(row == place(), gate[pl.ds(n, 1), :], 0.0).astype(jnp.bfloat16)

    def turned(zz):
        bytes_of(cb.at[zz], r_o.at[zz]).wait()
        ctt[...] = cb[zz].T

    def tile(zz, t):
        rhs = tab[pl.ds(zz % 4 * 16, 16), :, t].reshape(16 * SLOTS, 256)
        return jnp.dot(ctt[...], rhs, preferred_element_type=jnp.float32)

    def tiles(body):
        @pl.loop(0, 4)
        def _(n):
            body(pl.ds(pl.multiple_of(n * 256, 256), 256))

    def r_copy(way, i):
        to = (right, left)[way]
        if i == 0:
            rows = slice(0, 128) if way == 0 else slice(128, 256)
            src, dst = rsend.at[0, 0, rows], rrecv.at[way, 0, rows]
        else:
            src, dst = rsend.at[way, i], rrecv.at[way, i]
        return remote(src, dst, s_r.at[way, i], r_r.at[way, i], to)

    for i in range(4):
        pending += [r_copy(0, i).wait_send, r_copy(1, i).wait_send]
    far = (z + 4) % 8
    turned(far)

    def start_far(t):
        rsend[0, 0, :, t] = tile(far, t).astype(jnp.bfloat16)

    tiles(start_far)
    r_copy(0, 0).start()
    r_copy(1, 0).start()
    for i in range(1, 4):
        for way in range(2):
            zz = (z + 4 - i) % 8 if way == 0 else (z + 4 + i) % 8
            turned(zz)

            def keep(t, zz=zz):
                acc[:, t] = tile(zz, t)

            def add(t, way=way, i=i):
                rsend[way, i, :, t] = (
                    acc[:, t] + rrecv[way, i - 1, :, t].astype(jnp.float32)
                ).astype(jnp.bfloat16)

            tiles(keep)
            r_copy(way, i - 1).wait_recv()
            tiles(add)
            r_copy(way, i).start()
    turned(z)
    hid_over().wait_recv()

    def start(t, before):
        base[t, :] = before + tile(z, t).T

    @pl.loop(0, 2)
    def _(n):
        rows = pl.ds(pl.multiple_of(n * 256, 256), 256)
        start(pl.ds(pl.multiple_of(z_hi * 512 + n * 256, 256), 256), hid[0, rows, :])
        start(
            pl.ds(pl.multiple_of((1 - z_hi) * 512 + n * 256, 256), 256),
            hm[rows, :].astype(jnp.float32),
        )

    r_copy(0, 3).wait_recv()
    r_copy(1, 3).wait_recv()

    @tiles
    def _(t):
        arrived = rrecv[0, 3, :, t].astype(jnp.float32) + rrecv[1, 3, :, t].astype(jnp.float32)
        out_ref[t, :] = (base[t, :] + arrived.T).astype(jnp.bfloat16)


    for check in pending:
        check()


def shards(q, k, v, residual, w, gain, gate_up, down, ids, gates):
    vmem = pl.BlockSpec(memory_space=pltpu.VMEM)
    anywhere = pl.BlockSpec(memory_space=pl.ANY)
    bf16, f32 = jnp.bfloat16, jnp.float32
    dma = pltpu.SemaphoreType.DMA
    out = pl.pallas_call(
        whole,
        out_shape=jax.ShapeDtypeStruct((LENGTH, BLK), bf16),
        in_specs=[vmem] * 8 + [anywhere] * 2,
        out_specs=vmem,
        scratch_shapes=[
            pltpu.VMEM((2, LENGTH, 256), bf16),
            pltpu.VMEM((8, 16 * SLOTS, BLK), bf16),
            pltpu.VMEM((4, TOP, LENGTH), jnp.int32),
            pltpu.VMEM((4, TOP, LENGTH), f32),
            pltpu.VMEM((64, LENGTH), f32),
            pltpu.VMEM((64, LENGTH), f32),
            pltpu.VMEM((64, SLOTS, LENGTH), bf16),
            pltpu.VMEM((2, 8, 512, BLK), bf16),
            pltpu.VMEM((8, 16 * SLOTS, BLK), bf16),
            pltpu.VMEM((16 * SLOTS, D), bf16),
            pltpu.VMEM((2, D, 768), bf16),
            pltpu.VMEM((2, 384, D), bf16),
            pltpu.VMEM((2, 512, BLK), f32),
            pltpu.VMEM((4, 1, 512), f32),
            pltpu.VMEM((BLK, 16 * SLOTS), bf16),
            pltpu.VMEM((2, 4, BLK, LENGTH), bf16),
            pltpu.VMEM((2, 4, BLK, LENGTH), bf16),
            pltpu.VMEM((D, BLK), bf16),
            pltpu.VMEM((512, BLK), bf16),
            pltpu.VMEM((1, BLK), f32),
            pltpu.VMEM((512, BLK), bf16),
            pltpu.VMEM((512, BLK), bf16),
            pltpu.VMEM((BLK, LENGTH), f32),
            pltpu.VMEM((LENGTH, BLK), f32),
            dma((8,)), dma((8,)), dma((2, 4)), dma((2, 4)), dma((3,)), dma((2,)), dma((3,)), dma((3,)),
            dma((2, 4)), dma((2, 4)),
            dma((8,)), dma((8,)), dma((4,)), dma((6,)), dma((2,)), dma((2,)), dma((2,)),
            dma((2, 4, 2)), dma((2, 4, 2)), dma((8,)), dma((2,)), dma((2, 2)), dma((8,)),
            dma((2, 4)), dma((2, 4)),
        ],
        compiler_params=pltpu.CompilerParams(
            collective_id=0, has_side_effects=True, vmem_limit_bytes=63 * 1024 * 1024
        ),
    )(
        q[0], k[0], v[0], residual[0], w, gain[None], ids[0].T, gates[0].T,
        gate_up[0], down[0],
    )
    return out[None]


def solution(mesh):
    return jax.shard_map(
        shards,
        mesh=mesh,
        in_specs=(
            P("exp", "ctx", None),
            P("exp", "ctx", None),
            P("exp", "ctx", None),
            P("exp", None, "ctx"),
            P(None, "ctx"),
            P("ctx"),
            P(("ctx", "exp"), None, None),
            P(("ctx", "exp"), None, None),
            P("exp", None, None),
            P("exp", None, None),
        ),
        out_specs=P("exp", None, "ctx"),
        check_vma=False,
    )
```

```python
import jax
import jax.numpy as jnp
from jax import lax
from jax.experimental import pallas as pl
from jax.experimental.pallas import tpu as pltpu
from jax.sharding import PartitionSpec as P

LENGTH = 1024
D = 2048
HEAD = 128
TOP = 8
SLOTS = 80
BLK = 256
MESH = pl.DeviceIdType.MESH
norm_eps = 1e-06


def whole(
    q_ref, k_ref, v_ref, res_ref, w_ref, gain_ref, ids_ref, gates_ref, gu_ref, dp_ref,
    out_ref,
    kvb, cb, idb, gtb, rank, gate, tab, xb, sb, rb, gw, dw, hid, sq, ctt, rsend, rrecv, wm, resm, gm, hs, hm, acc, base,
    s_kv, r_kv, s_cx, r_cx, s_wm, r_wm, s_rm, r_rm, s_id, r_id, s_sq, r_sq, s_w, r_w, l_w, s_c, r_c2,
    s_z, r_z, s_f, r_f, s_o, r_o, s_r, r_r,
):
    ctx = lax.axis_index("ctx")
    exp = lax.axis_index("exp")
    z_hi, y = ctx // 4, ctx % 4
    z_lo, j = exp // 8, exp % 8
    x, core = j // 2, j % 2
    z = z_hi * 4 + z_lo
    mirror = (z_hi + 1) % 2 * 4 + y

    def at_z(to):
        return ((to // 4) * 4 + y, (to % 4) * 8 + j)

    def remote(src, dst, send, recv, where):
        return pltpu.make_async_remote_copy(
            src_ref=src, dst_ref=dst, send_sem=send, recv_sem=recv,
            device_id=where, device_id_type=MESH,
        )

    def bytes_of(ref, sem):
        return pltpu.make_async_copy(ref, ref, sem)

    barrier = pltpu.get_barrier_semaphore()
    pending = []

    def greet(where):
        pl.semaphore_signal(barrier, inc=1, device_id=where, device_id_type=MESH)

    @pl.loop(0, 32)
    def _(n):
        yy, jj = n // 8, n % 8

        @pl.when(jnp.logical_or(yy != y, jj != j))
        def _():
            greet((z_hi * 4 + yy, z_lo * 8 + jj))

    @pl.loop(1, 8)
    def _(n):
        greet(at_z((z + n) % 8))

    pl.semaphore_wait(barrier, 31 + 7)

    def id_copies(n):
        to = (ctx, (z_lo + n) % 4 * 8 + j)
        return (
            remote(ids_ref, idb.at[z_lo], s_id.at[0, n], r_id.at[0, z_lo], to),
            remote(gates_ref, gtb.at[z_lo], s_id.at[1, n], r_id.at[1, z_lo], to),
        )

    own = pl.ds(pl.multiple_of(ctx * 128, 128), 128)
    kvb[0, own, :] = k_ref[...]
    kvb[1, own, :] = v_ref[...]

    def kv_copy(slot, n, sem):
        rows = pl.ds(pl.multiple_of(slot * 128, 128), 128)
        part = kvb.at[:, rows, :]
        return remote(part, part, s_kv.at[sem], r_kv.at[slot], (z_hi * 4 + (y + n) % 4, exp))

    def kv_over():
        part = kvb.at[:, own, :]
        return remote(part, part, s_kv.at[0], r_kv.at[ctx], (mirror, exp))

    @pl.when(z_hi == 0)
    def _():
        kv_over().start()
        kvb[:, 512:1024, :] = jnp.zeros((2, 512, 256), jnp.bfloat16)

    for n in (1, 2, 3):
        kv_copy(ctx, n, n).start()
    for n in (1, 2, 3):
        for copy in id_copies(n):
            copy.start()
    idb[z_lo] = ids_ref[...]
    gtb[z_lo] = gates_ref[...]

    def kv_sent():
        @pl.when(z_hi == 0)
        def _():
            kv_over().wait_send()

        for n in (1, 2, 3):
            kv_copy(ctx, n, n).wait_send()
            for copy in id_copies(n):
                copy.wait_send()

    pending.append(kv_sent)

    half_w = pl.ds(pl.multiple_of(core * 1024, 1024), 1024)
    here = pl.ds(pl.multiple_of(z_hi * 512, 512), 512)
    there = pl.ds(pl.multiple_of((1 - z_hi) * 512, 512), 512)
    other = (mirror, exp)

    def w_over(n):
        to = (mirror, jnp.where(z_lo == 3, n, 3 - n) * 8 + j)
        return remote(w_ref.at[half_w, :], wm.at[half_w, :], s_wm.at[n], r_wm.at[0], to)

    def w_sibling():
        return remote(
            wm.at[half_w, :], wm.at[half_w, :], s_wm.at[2], r_wm.at[1], (ctx, exp + 1 - 2 * core)
        )

    def res_over():
        return (
            remote(res_ref.at[there, :], resm, s_rm.at[0], r_rm.at[0], other),
            remote(gain_ref, gm, s_rm.at[1], r_rm.at[1], other),
        )

    def w_sent():
        @pl.when(jnp.logical_or(z_lo == 3, z_lo == 0))
        def _():
            w_over(0).wait_send()
            w_over(1).wait_send()

        w_sibling().wait_send()
        for copy in res_over():
            copy.wait_send()

    pending.append(w_sent)

    mine = core == y % 2
    sibling = (ctx, exp + 1 - 2 * core)
    across = (ctx + 1 - 2 * (y % 2), exp)

    def own_local():
        return (
            pltpu.make_async_copy(gu_ref, gw.at[0], l_w.at[0]),
            pltpu.make_async_copy(dp_ref, dw.at[0], l_w.at[1]),
        )

    def own_sibling():
        return (
            remote(gu_ref, gw.at[0], s_w.at[0], r_w.at[0], sibling),
            remote(dp_ref, dw.at[0], s_w.at[1], r_w.at[1], sibling),
        )

    cuts = (0, 1024, 1280, 2048)

    def own_across(n):
        if n == 3:
            return remote(dp_ref, dw.at[1], s_w.at[3], r_w.at[5], across)
        rows = slice(cuts[n], cuts[n + 1])
        return remote(gu_ref.at[rows], gw.at[1, rows], s_w.at[n], r_w.at[2 + n], across)

    def across_arrived():
        for n in range(3):
            bytes_of(gw.at[1, cuts[n] : cuts[n + 1]], r_w.at[2 + n]).wait()
        bytes_of(dw.at[1], r_w.at[5]).wait()

    def send_across(*which):
        @pl.when(jnp.logical_not(mine))
        def _():
            for n in which:
                own_across(n).start()

    def pass_sibling():
        return (
            remote(gw.at[1], gw.at[1], s_c.at[0], r_c2.at[0], sibling),
            remote(dw.at[1], dw.at[1], s_c.at[1], r_c2.at[1], sibling),
        )

    @pl.when(mine)
    def _():
        for copy in own_local() + own_sibling():
            copy.start()

    send_across(0)

    def weights_sent():
        @pl.when(mine)
        def _():
            for copy in own_sibling():
                copy.wait_send()

        @pl.when(jnp.logical_not(mine))
        def _():
            for n in range(4):
                own_across(n).wait_send()

    pending.append(weights_sent)

    rrecv[0, 0, 128:256, :] = jnp.zeros((128, LENGTH), jnp.bfloat16)
    rrecv[1, 0, 0:128, :] = jnp.zeros((128, LENGTH), jnp.bfloat16)

    for n in (1, 2, 3):
        at = (z_lo + n) % 4
        bytes_of(idb.at[at], r_id.at[0, at]).wait()
        bytes_of(gtb.at[at], r_id.at[1, at]).wait()

    @pl.when(jnp.logical_or(z_lo == 3, z_lo == 0))
    def _():
        w_over(0).start()
        w_over(1).start()

    @pl.when(z_hi == 1)
    def _():
        for copy in res_over():
            copy.start()

    @pl.loop(0, 4)
    def _(s):
        number = lax.broadcasted_iota(jnp.int32, (16, LENGTH), 0)
        number = z_hi * 64 + z_lo * 8 + jnp.where(number >= 8, number + 24, number)
        found = jnp.zeros((16, LENGTH), jnp.float32)
        weight = jnp.zeros((16, LENGTH), jnp.float32)
        ids, gates = idb[s], gtb[s]
        for k in range(TOP):
            same = ids[k : k + 1, :] == number
            found = found + jnp.where(same, 1.0, 0.0)
            weight = weight + jnp.where(same, gates[k : k + 1, :], 0.0)
        rows = pl.ds(pl.multiple_of(s * 16, 16), 16)
        rank[rows, :] = found
        gate[rows, :] = weight

    members = rank[...]
    members16 = members.astype(jnp.bfloat16)
    before = []
    for b in range(8):
        row = lax.broadcasted_iota(jnp.int32, (LENGTH, 128), 0)
        column = lax.broadcasted_iota(jnp.int32, (LENGTH, 128), 1) + b * 128
        earlier = jnp.where(row < column, 1.0, 0.0).astype(jnp.bfloat16)
        before.append(jnp.dot(members16, earlier, preferred_element_type=jnp.float32))
    rank[...] = jnp.where(members > 0.5, jnp.concatenate(before, axis=1), -1.0)

    place = lambda: lax.broadcasted_iota(jnp.int32, (SLOTS, LENGTH), 0).astype(jnp.float32)

    @pl.loop(0, 64)
    def _(n):
        row = rank[pl.ds(n, 1), :]
        tab[n] = jnp.where(row == place(), 1.0, 0.0).astype(jnp.bfloat16)

    @pl.when(z_hi == 1)
    def _():
        bytes_of(kvb.at[:, pl.ds(0, 128), :], r_kv.at[mirror]).wait()
        for n in (1, 2, 3):
            kv_copy(mirror, n, 3 + n).start()

    def kv_passed():
        @pl.when(z_hi == 1)
        def _():
            for n in (1, 2, 3):
                kv_copy(mirror, n, 3 + n).wait_send()

    pending.append(kv_passed)

    for n in (1, 2, 3):
        bytes_of(kvb.at[:, pl.ds(0, 128), :], r_kv.at[z_hi * 4 + (y + n) % 4]).wait()

    @pl.when(z_hi == 1)
    def _():
        for n in (1, 2, 3):
            bytes_of(kvb.at[:, pl.ds(0, 128), :], r_kv.at[(y + n) % 4]).wait()

    send_across(1)

    @pl.when(z_hi == 0)
    def _():
        for copy in res_over():
            copy.start()

    def cx_part(g, n, first=0, count=4):
        rows = pl.ds(pl.multiple_of((y + n) % 4 * 128, 128), 128)
        return cb.at[pl.ds(4 * g + first, count), rows, :]

    def cx_copy(g, way):
        if way < 2:
            part = cx_part(g, 0)
        elif way == 2:
            part = cx_part(g, 3, 0, 2)
        else:
            part = cx_part(g, 1, 2, 2)
        to = (z_hi * 4 + (y + (1 if way % 2 == 0 else 3)) % 4, exp)
        return remote(part, part, s_cx.at[g, way], r_cx.at[g, way], to)

    for g in range(2):
        lanes = slice(g * 128, g * 128 + 128)

        @pl.loop(0, 4)
        def _(n):
            results = []
            for i in range(2):
                cols = pl.ds(pl.multiple_of((g * 8 + n * 2 + i) * 128, 128), 128)
                scores = lax.dot_general(
                    q_ref[:, cols], kvb[0, :, lanes], (((1,), (1,)), ((), ())),
                    preferred_element_type=jnp.float32,
                ) * (HEAD**-0.5)
                row = lax.broadcasted_iota(jnp.int32, (128, LENGTH), 0) + ctx * 128
                column = lax.broadcasted_iota(jnp.int32, (128, LENGTH), 1)
                scores = jnp.where(column <= row, scores, -1e30)
                top = jnp.max(scores, axis=1, keepdims=True)
                weights = jnp.exp(scores - top)
                total = jnp.sum(weights, axis=1, keepdims=True)
                mixed = jnp.dot(
                    weights.astype(jnp.bfloat16), kvb[1, :, lanes],
                    preferred_element_type=jnp.float32,
                )
                results.append((mixed / total).astype(jnp.bfloat16))
            cb[g * 4 + n, pl.ds(pl.multiple_of(y * 128, 128), 128), :] = jnp.concatenate(results, axis=1)

        cx_copy(g, 0).start()
        cx_copy(g, 1).start()

    for g in range(2):
        for way in range(2):
            cx_copy(g, way).wait_recv()
            cx_copy(g, 2 + way).start()
    bytes_of(wm.at[half_w, :], r_wm.at[0]).wait()
    w_sibling().start()
    for g in range(2):
        for way in (2, 3):
            cx_copy(g, way).wait_recv()

    bytes_of(resm, r_rm.at[0]).wait()
    bytes_of(gm, r_rm.at[1]).wait()
    bytes_of(wm.at[half_w, :], r_wm.at[1]).wait()
    for b in range(2):
        rows = slice(b * 256, b * 256 + 256)
        mine_rows = pl.ds(pl.multiple_of(z_hi * 512 + b * 256, 256), 256)
        squares = jnp.zeros((256, 128), jnp.float32)
        for side, weight in enumerate((w_ref, wm)):
            total = (res_ref[mine_rows, :] if side == 0 else resm[rows, :]).astype(jnp.float32)
            for f in range(8):
                total = total + jnp.dot(
                    cb[f, rows, :], weight[f * BLK : f * BLK + BLK, :],
                    preferred_element_type=jnp.float32,
                )
            hid[side, rows, :] = total
            squared = total * total
            squares = squares + (squared[:, :128] + squared[:, 128:])
        sq[y, :, rows] = jnp.sum(squares.T, axis=0, keepdims=True)

    def sq_copy(n):
        to = (z_hi * 4 + (y + n) % 4, exp)
        return remote(sq.at[y], sq.at[y], s_sq.at[n], r_sq.at[y], to)

    for n in (1, 2, 3):
        sq_copy(n).start()
        pending.append(sq_copy(n).wait_send)
    send_across(2, 3)
    hs[...] = hid[1].astype(jnp.bfloat16)
    for n in (1, 2, 3):
        at = (y + n) % 4
        bytes_of(sq.at[at], r_sq.at[at]).wait()
    total = sq[0] + sq[1] + (sq[2] + sq[3])
    inverse = lax.rsqrt(total / D + norm_eps)
    for b in range(2):
        rows = slice(b * 256, b * 256 + 256)
        column = jnp.broadcast_to(inverse[:, rows], (128, 256)).T
        column = jnp.concatenate([column, column], axis=1)
        for side, gains in enumerate((gain_ref, gm)):
            xb[z_hi if side == 0 else 1 - z_hi, z, rows, :] = (
                hid[side, rows, :] * column * gains[...]
            ).astype(jnp.bfloat16)

    def hid_over():
        return remote(hs, hm, s_rm.at[2], r_rm.at[2], other)

    right, left = at_z((z + 1) % 8), at_z((z + 7) % 8)

    def z_copy(way, i, half):
        block = (z + 8 - i) % 8 if way == 0 else (z + i) % 8
        part = xb.at[half, block]
        if i == 3:
            part = part.at[0:256] if way == 0 else part.at[256:512]
        to = (right, left)[way]
        return remote(part, part, s_z.at[way, i, half], r_z.at[way, i, half], to)

    def is_me(s, yy, xx):
        return jnp.logical_and(s % 2 == core, jnp.logical_and(yy == y, xx == x))

    def deal(s, half):
        to_rows = pl.ds(pl.multiple_of((s // 2 * 8 + j) * SLOTS, SLOTS), SLOTS)
        dst = rb.at[to_rows, pl.ds(pl.multiple_of((half * 4 + y) * BLK, BLK), BLK)]
        zz = half * 4 + s

        @pl.loop(0, 4)
        def _(turn):
            n = (turn + y // 2 * 2 + x // 2) % 4
            lhs = tab[pl.ds(s * 16 + n * 4, 4)].reshape(4 * SLOTS, LENGTH)
            rows = pl.ds(pl.multiple_of(n * 4 * SLOTS, 4 * SLOTS), 4 * SLOTS)
            sb[zz, rows, :] = (
                jnp.dot(lhs[:, :512], xb[half, s], preferred_element_type=jnp.float32)
                + jnp.dot(lhs[:, 512:], xb[half, 4 + s], preferred_element_type=jnp.float32)
            ).astype(jnp.bfloat16)

            @pl.loop(0, 4)
            def _(i):
                e = n * 4 + (i + x % 2 * 2 + y % 2) % 4
                yy, xx = e // 8 * 2 + e % 2, e % 8 // 2
                src = sb.at[zz, pl.ds(pl.multiple_of(e * SLOTS, SLOTS), SLOTS), :]
                same = is_me(s, yy, xx)

                @pl.when(same)
                def _():
                    pltpu.make_async_copy(src, dst, r_f.at[s // 2]).start()

                @pl.when(jnp.logical_not(same))
                def _():
                    to = (z_hi * 4 + yy, z_lo * 8 + xx * 2 + s % 2)
                    remote(src, dst, s_f.at[zz], r_f.at[s // 2], to).start()

    for half in range(2):
        for way in range(2):
            z_copy(way, 0, half).start()
            pending += [z_copy(way, i, half).wait_send for i in range(4)]
    for g in range(2):
        for way in range(4):
            cx_copy(g, way).wait_send()
    for i in range(3):
        for half in range(2):
            for way in range(2):
                z_copy(way, i, half).wait_recv()
                z_copy(way, i + 1, half).start()
            if i == 1:
                deal((z_lo + 2) % 4, half)
            if i == 2:
                deal((z_lo + 1) % 4, half)
    for half in range(2):
        z_copy(0, 3, half).wait_recv()
        z_copy(1, 3, half).wait_recv()
        deal(z_lo, half)
    for half in range(2):
        deal((z_lo + 3) % 4, half)
    hid_over().start()
    pending.append(hid_over().wait_send)

    @pl.when(mine)
    def _():
        across_arrived()
        for copy in pass_sibling():
            copy.start()

    def weights_passed():
        @pl.when(mine)
        def _():
            for copy in pass_sibling():
                copy.wait_send()

    pending.append(weights_passed)
    @pl.when(mine)
    def _():
        for copy in own_local():
            copy.wait()

    @pl.when(jnp.logical_not(mine))
    def _():
        for n in (0, 1):
            bytes_of((gw, dw)[n].at[0], r_w.at[n]).wait()
            bytes_of((gw, dw)[n].at[1], r_c2.at[n]).wait()

    def dealt():
        @pl.loop(0, 8)
        def _(zz):
            some = (zz % 4) % 2 == core

            @pl.when(some)
            def _():
                bytes_of(sb.at[zz, 0 : 15 * SLOTS], s_f.at[zz]).wait()

            @pl.when(jnp.logical_not(some))
            def _():
                bytes_of(sb.at[zz], s_f.at[zz]).wait()

    pending.append(dealt)

    def distance(zz):
        up = (zz + 8 - z) % 8
        return jnp.minimum(up, 8 - up)

    my_e = y // 2 * 8 + x * 2 + y % 2

    def send_back(p, half, n):
        slot = half * 4 + 2 * p + core
        dst = cb.at[slot, pl.ds(pl.multiple_of(my_e * SLOTS, SLOTS), SLOTS), :]

        @pl.loop(0, 16)
        def _(m):
            yy, jj = (m + y) % 4, n * 4 + (m // 4 + x % 2 * 2 + core) % 4
            from_rows = pl.ds(pl.multiple_of((p * 8 + jj) * SLOTS, SLOTS), SLOTS)
            col = pl.ds(pl.multiple_of((half * 4 + yy) * BLK, BLK), BLK)
            src = rb.at[from_rows, col]
            same = jnp.logical_and(yy == y, jj == j)

            @pl.when(same)
            def _():
                pltpu.make_async_copy(src, dst, r_o.at[slot]).start()

            @pl.when(jnp.logical_not(same))
            def _():
                to = (z_hi * 4 + yy, z_lo * 8 + jj)
                remote(src, dst, s_o.at[p, half], r_o.at[slot], to).start()

    plain = core == z_lo % 2

    def far_half(p):
        s = 2 * p + core
        return jnp.where(distance(s) >= distance(4 + s), 0, 1)

    for turn in range(2):
        p = (z_lo // 2 + 1 + turn) % 2
        bytes_of(rb.at[pl.ds(pl.multiple_of(p * 640, 640), 640)], r_f.at[p]).wait()

        @pl.loop(0, 2)
        def _(m):
            n = (m + x // 2) % 2
            rows = pl.ds(pl.multiple_of(p * 640 + n * 320, 320), 320)
            units = []
            for h in range(2):
                u = jnp.dot(rb[rows, :], gw[h], preferred_element_type=jnp.float32)
                v = u[:, :384]
                units.append((v / (1.0 + jnp.exp(-v)) * u[:, 384:]).astype(jnp.bfloat16))

            def results(half):
                for i in range(4):
                    cols = pl.ds(pl.multiple_of((half * 4 + i) * BLK, BLK), BLK)
                    rb[rows, cols] = (
                        jnp.dot(units[0], dw[0, :, cols], preferred_element_type=jnp.float32)
                        + jnp.dot(units[1], dw[1, :, cols], preferred_element_type=jnp.float32)
                    ).astype(jnp.bfloat16)

            first = far_half(p)
            results(first)
            if turn == 1:
                send_back(p, first, n)
            else:

                @pl.when(jnp.logical_not(plain))
                def _():
                    send_back(p, first, n)

            results(1 - first)

    def send_both(p, half):
        @pl.loop(0, 2)
        def _(m):
            send_back(p, half, (m + x // 2) % 2)

    early, late = (z_lo // 2 + 1) % 2, z_lo // 2

    @pl.when(plain)
    def _():
        send_both(early, far_half(early))

    send_both(early, 1 - far_half(early))
    send_both(late, 1 - far_half(late))

    for p in range(2):
        for half in range(2):
            pending.append(bytes_of(sb.at[0:5, 0:496], s_o.at[p, half]).wait)

    @pl.loop(0, 64)
    def _(n):
        row = rank[pl.ds(n, 1), :]
        tab[n] = jnp.where(row == place(), gate[pl.ds(n, 1), :], 0.0).astype(jnp.bfloat16)

    def turned(zz):
        bytes_of(cb.at[zz], r_o.at[zz]).wait()
        ctt[...] = cb[zz].T

    def tile(zz, t):
        rhs = tab[pl.ds(zz % 4 * 16, 16), :, t].reshape(16 * SLOTS, 256)
        return jnp.dot(ctt[...], rhs, preferred_element_type=jnp.float32)

    def tiles(body):
        @pl.loop(0, 4)
        def _(n):
            body(pl.ds(pl.multiple_of(n * 256, 256), 256))

    def r_copy(way, i):
        to = (right, left)[way]
        if i == 0:
            rows = slice(0, 128) if way == 0 else slice(128, 256)
            src, dst = rsend.at[0, 0, rows], rrecv.at[way, 0, rows]
        else:
            src, dst = rsend.at[way, i], rrecv.at[way, i]
        return remote(src, dst, s_r.at[way, i], r_r.at[way, i], to)

    for i in range(4):
        pending += [r_copy(0, i).wait_send, r_copy(1, i).wait_send]
    far = (z + 4) % 8
    turned(far)

    def start_far(t):
        rsend[0, 0, :, t] = tile(far, t).astype(jnp.bfloat16)

    tiles(start_far)
    r_copy(0, 0).start()
    r_copy(1, 0).start()
    for i in range(1, 4):
        for way in range(2):
            zz = (z + 4 - i) % 8 if way == 0 else (z + 4 + i) % 8
            turned(zz)

            def keep(t, zz=zz):
                acc[:, t] = tile(zz, t)

            def add(t, way=way, i=i):
                rsend[way, i, :, t] = (
                    acc[:, t] + rrecv[way, i - 1, :, t].astype(jnp.float32)
                ).astype(jnp.bfloat16)

            tiles(keep)
            r_copy(way, i - 1).wait_recv()
            tiles(add)
            r_copy(way, i).start()
    turned(z)
    hid_over().wait_recv()

    def start(t, before):
        base[t, :] = before + tile(z, t).T

    @pl.loop(0, 2)
    def _(n):
        rows = pl.ds(pl.multiple_of(n * 256, 256), 256)
        start(pl.ds(pl.multiple_of(z_hi * 512 + n * 256, 256), 256), hid[0, rows, :])
        start(
            pl.ds(pl.multiple_of((1 - z_hi) * 512 + n * 256, 256), 256),
            hm[rows, :].astype(jnp.float32),
        )

    r_copy(0, 3).wait_recv()
    r_copy(1, 3).wait_recv()

    @tiles
    def _(t):
        arrived = rrecv[0, 3, :, t].astype(jnp.float32) + rrecv[1, 3, :, t].astype(jnp.float32)
        out_ref[t, :] = (base[t, :] + arrived.T).astype(jnp.bfloat16)


    for check in pending:
        check()


def shards(q, k, v, residual, w, gain, gate_up, down, ids, gates):
    vmem = pl.BlockSpec(memory_space=pltpu.VMEM)
    anywhere = pl.BlockSpec(memory_space=pl.ANY)
    bf16, f32 = jnp.bfloat16, jnp.float32
    dma = pltpu.SemaphoreType.DMA
    out = pl.pallas_call(
        whole,
        out_shape=jax.ShapeDtypeStruct((LENGTH, BLK), bf16),
        in_specs=[vmem] * 8 + [anywhere] * 2,
        out_specs=vmem,
        scratch_shapes=[
            pltpu.VMEM((2, LENGTH, 256), bf16),
            pltpu.VMEM((8, 16 * SLOTS, BLK), bf16),
            pltpu.VMEM((4, TOP, LENGTH), jnp.int32),
            pltpu.VMEM((4, TOP, LENGTH), f32),
            pltpu.VMEM((64, LENGTH), f32),
            pltpu.VMEM((64, LENGTH), f32),
            pltpu.VMEM((64, SLOTS, LENGTH), bf16),
            pltpu.VMEM((2, 8, 512, BLK), bf16),
            pltpu.VMEM((8, 16 * SLOTS, BLK), bf16),
            pltpu.VMEM((16 * SLOTS, D), bf16),
            pltpu.VMEM((2, D, 768), bf16),
            pltpu.VMEM((2, 384, D), bf16),
            pltpu.VMEM((2, 512, BLK), f32),
            pltpu.VMEM((4, 1, 512), f32),
            pltpu.VMEM((BLK, 16 * SLOTS), bf16),
            pltpu.VMEM((2, 4, BLK, LENGTH), bf16),
            pltpu.VMEM((2, 4, BLK, LENGTH), bf16),
            pltpu.VMEM((D, BLK), bf16),
            pltpu.VMEM((512, BLK), bf16),
            pltpu.VMEM((1, BLK), f32),
            pltpu.VMEM((512, BLK), bf16),
            pltpu.VMEM((512, BLK), bf16),
            pltpu.VMEM((BLK, LENGTH), f32),
            pltpu.VMEM((LENGTH, BLK), f32),
            dma((8,)), dma((8,)), dma((2, 4)), dma((2, 4)), dma((3,)), dma((2,)), dma((3,)), dma((3,)),
            dma((2, 4)), dma((2, 4)),
            dma((8,)), dma((8,)), dma((4,)), dma((6,)), dma((2,)), dma((2,)), dma((2,)),
            dma((2, 4, 2)), dma((2, 4, 2)), dma((8,)), dma((2,)), dma((2, 2)), dma((8,)),
            dma((2, 4)), dma((2, 4)),
        ],
        compiler_params=pltpu.CompilerParams(
            collective_id=0, has_side_effects=True, vmem_limit_bytes=63 * 1024 * 1024
        ),
    )(
        q[0], k[0], v[0], residual[0], w, gain[None], ids[0].T, gates[0].T,
        gate_up[0], down[0],
    )
    return out[None]


def solution(mesh):
    return jax.shard_map(
        shards,
        mesh=mesh,
        in_specs=(
            P("exp", "ctx", None),
            P("exp", "ctx", None),
            P("exp", "ctx", None),
            P("exp", None, "ctx"),
            P(None, "ctx"),
            P("ctx"),
            P(("ctx", "exp"), None, None),
            P(("ctx", "exp"), None, None),
            P("exp", None, None),
            P("exp", None, None),
        ),
        out_specs=P("exp", None, "ctx"),
        check_vma=False,
    )
```
